256 devices in a mesh: blk: 256 (over y, z, x, core).
Axes of the slice: x: 4, y: 4, z: 8, core: 2. Of those that a mesh axis runs over, the one named last changes fastest.
Arguments:
- image: bfloat16 [131072, 1152], P('blk'), may hold values from -2 to 2
- text: bfloat16 [131072, 1152], P('blk'), may hold values from -2 to 2
- scale: float32 [1], replicated, may hold values from 4 to 16
- bias: float32 [1], replicated, may hold values from -4 to -1
Outputs:
- grad_image: float32 [131072, 1152], P('blk')
- grad_text: float32 [131072, 1152], P('blk')
The draws below stay inside these ranges and needn't reach their ends.
All inputs are finite; a program needn't handle non-finite values.
Results may differ from the reference program's by a relative error of at most 0.0046.
Values may be sent and summed in bfloat16 or wider, within the bound.
A program may use at most 64 MiB of HBM per device.

```python
import jax
import jax.numpy as jnp
from jax import lax

D = 1152
ROWS = 512
STEPS = 4
TOKENS = 131072
N_BLK = 256


def common_part(key):
    return jax.random.normal(key, (TOKENS, D), jnp.float32)


def embed_rows(key, shared):
    first, second = jax.random.split(key, 2)
    noise = jax.random.normal(first, (TOKENS, D), jnp.float32)
    mixed = jnp.clip(0.7 * shared + 0.7 * noise, -6.0, 6.0)
    row_scale = jnp.exp(jax.random.uniform(second, (TOKENS, 1), jnp.float32, 0.0, 2.302585))
    return (mixed * row_scale / 34.0).astype(jnp.bfloat16)


def draw_image(key, part):
    shared = common_part(key)
    key = jax.random.fold_in(key, 11)
    return embed_rows(key, shared)


def draw_text(key, part):
    shared = common_part(key)
    key = jax.random.fold_in(key, 23)
    return embed_rows(key, shared)


def setup_inputs(seed: int = 0) -> dict:
    key_of = jax.random.split(jax.random.key(seed), 5)
    return {
        "image": draw_image(jax.random.fold_in(key_of[4], 71), 0),
        "text": draw_text(jax.random.fold_in(key_of[4], 71), 0),
        "scale": jnp.clip(jax.random.uniform(key_of[2], (1,), jnp.float32, 4.0, 16.0), 4.0, 16.0),
        "bias": jnp.clip(jax.random.uniform(key_of[3], (1,), jnp.float32, -4.0, -1.0), -4.0, -1.0),
    }


def normalize(values):
    wide = values.astype(jnp.float32)
    norms = jnp.sqrt(lax.optimization_barrier(jnp.sum(wide * wide, axis=-1, keepdims=True)) + 1e-06)
    return (wide / norms, norms)

def norm_back(grad_unit, unit, norms):
    inner = lax.optimization_barrier(jnp.sum(unit * grad_unit, axis=-1, keepdims=True))
    return (grad_unit - unit * inner) / norms

def reference(image, text, scale, bias):
    factor = scale[0]
    offset = bias[0]
    unit_image, image_norm = normalize(image)
    unit_text, text_norm = normalize(text)
    image_low = unit_image.astype(jnp.bfloat16).reshape(N_BLK, ROWS, D).astype(jnp.float32)
    text_low = unit_text.astype(jnp.bfloat16).reshape(N_BLK, ROWS, D).astype(jnp.float32)
    labels = (jnp.arange(ROWS)[:, None] == jnp.arange(ROWS)[None, :]).astype(jnp.float32)
    grad_unit_image = jnp.zeros((N_BLK, ROWS, D), jnp.float32)
    grad_unit_text = jnp.zeros((N_BLK, ROWS, D), jnp.float32)
    for step in range(STEPS):
        partner = jnp.roll(text_low, step, axis=0)
        logits = factor * jnp.einsum('nrd,nsd->nrs', image_low, partner) + offset
        target = labels if step == 0 else jnp.zeros_like(labels)
        weights = (factor * (jax.nn.sigmoid(logits) - target)).astype(jnp.bfloat16).astype(jnp.float32)
        grad_unit_image = grad_unit_image + jnp.einsum('nrs,nsd->nrd', weights, partner)
        text_terms = jnp.einsum('nrs,nrd->nsd', weights, image_low)
        grad_unit_text = grad_unit_text + jnp.roll(text_terms, -step, axis=0)
    grad_image = norm_back(grad_unit_image.reshape(TOKENS, D), unit_image, image_norm)
    grad_text = norm_back(grad_unit_text.reshape(TOKENS, D), unit_text, text_norm)
    return (grad_image, grad_text)
```

```python
import functools

import jax
import jax.numpy as jnp
from jax import lax
from jax.experimental import pallas as pl
from jax.experimental.pallas import tpu as pltpu
from jax.sharding import PartitionSpec as P

MESH = pl.DeviceIdType.MESH
CHUNK = 128
TILE = 256
EPS = 1e-06


def inverse_norm(wide):
    return lax.rsqrt(jnp.sum(wide * wide, axis=-1, keepdims=True) + EPS)


def exchange(n, scale_ref, bias_ref, image_ref, text_ref, out_ref, x_raw, y_raw, x_low, y_low, x_sum, y_sum,
             passed, near, far, unit, load_sem, link_send, link_recv, pass_send, pass_recv, pair_send, pair_recv):
    rows, _ = x_raw.shape
    parts = rows // CHUNK
    me = lax.axis_index("blk")
    core = lax.rem(me, 2)
    partner = me + 1 - 2 * core
    ahead = lax.rem(me + 2 - 4 * core + n, n)
    behind = lax.rem(me - 2 + 4 * core + n, n)
    factor = scale_ref[0]
    offset = bias_ref[0]

    def load(x_ref, y_ref):
        pltpu.make_async_copy(y_ref, y_raw, load_sem.at[0]).start()
        pltpu.make_async_copy(x_ref, x_raw, load_sem.at[1]).start()

    pl.when(core == 0)(lambda: load(image_ref, text_ref))
    pl.when(core == 1)(lambda: load(text_ref, image_ref))

    barrier = pltpu.get_barrier_semaphore()
    for other in (partner, ahead, behind):
        pl.semaphore_signal(barrier, inc=1, device_id=(other,), device_id_type=MESH)
    pl.semaphore_wait(barrier, 3)

    def part(i):
        return pl.ds(pl.multiple_of(i * CHUNK, CHUNK), CHUNK)

    def link(src, i):
        return pltpu.make_async_remote_copy(
            src_ref=src, dst_ref=far.at[part(i)], send_sem=link_send.at[i], recv_sem=link_recv.at[i],
            device_id=(ahead,), device_id_type=MESH)

    def hand(i):
        return pltpu.make_async_remote_copy(
            src_ref=x_raw.at[part(i)], dst_ref=passed.at[part(i)], send_sem=pass_send.at[i], recv_sem=pass_recv.at[i],
            device_id=(partner,), device_id_type=MESH)

    def pair(src, i):
        return pltpu.make_async_remote_copy(
            src_ref=src, dst_ref=near.at[part(i)], send_sem=pair_send.at[i], recv_sem=pair_recv.at[i],
            device_id=(partner,), device_id_type=MESH)

    pltpu.make_async_copy(text_ref, y_raw, load_sem.at[0]).wait()
    for i in range(parts):
        link(y_raw.at[part(i)], i).start()
    pltpu.make_async_copy(text_ref, x_raw, load_sem.at[1]).wait()
    for i in range(parts):
        hand(i).start()
    for i in range(parts):
        pair(y_raw.at[part(i)], i).start()

    def meet(anchor, chunk, total, diagonal=None):
        for t in range(rows // TILE):
            tile = pl.ds(t * TILE, TILE)
            logits = factor * lax.dot_general(
                anchor[tile, :], chunk, (((1,), (1,)), ((), ())), preferred_element_type=jnp.float32) + offset
            probs = jax.nn.sigmoid(logits)
            if diagonal is not None:
                row = lax.broadcasted_iota(jnp.int32, probs.shape, 0) + t * TILE
                column = lax.broadcasted_iota(jnp.int32, probs.shape, 1) + diagonal
                probs = probs - (row == column).astype(jnp.float32)
            weights = (factor * probs).astype(jnp.bfloat16)
            total[tile, :] += jnp.dot(weights, chunk, preferred_element_type=jnp.float32)

    def low(src):
        wide = src[...].astype(jnp.float32)
        return (wide * inverse_norm(wide)).astype(jnp.bfloat16)

    def meet_raw(anchor, src, total):
        unit[...] = low(src)
        meet(anchor, unit[...], total)

    @pl.loop(0, parts)
    def _(i):
        here = part(i)
        x_low[here, :] = low(x_raw.at[here])
        y_low[here, :] = low(y_raw.at[here])
        x_sum[here, :] = jnp.zeros((CHUNK, x_sum.shape[1]), jnp.float32)
        y_sum[here, :] = jnp.zeros((CHUNK, y_sum.shape[1]), jnp.float32)

    @pl.loop(0, parts)
    def _(i):
        here = part(i)
        meet(x_low, y_low[here, :], x_sum, i * CHUNK)
        meet(y_low, x_low[here, :], y_sum, i * CHUNK)
        pair(y_raw.at[here], i).wait_recv()
        meet_raw(y_low, near.at[here], y_sum)

    @pl.loop(0, parts)
    def _(i):
        link(y_raw.at[part(i)], i).wait_recv()
        pair(far.at[part(i)], i + parts).start()
        hand(i).wait_recv()
        link(passed.at[part(i)], i + parts).start()
        meet_raw(x_low, far.at[part(i)], x_sum)
        pair(far.at[part(i)], i + parts).wait_recv()
        meet_raw(y_low, near.at[part(i + parts)], y_sum)

    @pl.loop(0, parts)
    def _(i):
        j = i + parts
        link(y_raw.at[part(i)], j).wait_recv()
        pair(far.at[part(j)], j + parts).start()
        link(far.at[part(j)], j + parts).start()
        meet_raw(x_low, far.at[part(j)], x_sum)
        pair(far.at[part(j)], j + parts).wait_recv()
        meet_raw(y_low, near.at[part(j + parts)], y_sum)

    def finish(raw, total, which):
        @pl.loop(0, parts)
        def _(i):
            here = part(i)
            wide = raw[here, :].astype(jnp.float32)
            inverse = inverse_norm(wide)
            own = wide * inverse
            grad = total[here, :]
            inner = jnp.sum(own * grad, axis=-1, keepdims=True)
            out_ref[which, here, :] = (grad - own * inner) * inverse

    finish(y_raw, y_sum, 1 - core)

    @pl.loop(0, parts)
    def _(i):
        j = i + 2 * parts
        link(y_raw.at[part(i)], j).wait_recv()
        meet_raw(x_low, far.at[part(j)], x_sum)

    finish(x_raw, x_sum, core)

    @pl.loop(0, parts)
    def _(i):
        hand(i).wait_send()

    @pl.loop(0, 3 * parts)
    def _(i):
        link(y_raw.at[part(0)], i).wait_send()
        pair(y_raw.at[part(0)], i).wait_send()


def solution(mesh):
    n = mesh.shape["blk"]

    def local(image, text, scale, bias):
        rows, width = image.shape
        parts = rows // CHUNK
        dma = pltpu.SemaphoreType.DMA
        both = pl.pallas_call(
            functools.partial(exchange, n),
            out_shape=pltpu.VMEM((2, rows, width), jnp.float32),
            in_specs=[pl.BlockSpec(memory_space=pltpu.SMEM)] * 2 + [pl.BlockSpec(memory_space=pl.ANY)] * 2,
            out_specs=pl.BlockSpec(memory_space=pltpu.VMEM),
            scratch_shapes=[
                pltpu.VMEM((rows, width), jnp.bfloat16),
                pltpu.VMEM((rows, width), jnp.bfloat16),
                pltpu.VMEM((rows, width), jnp.bfloat16),
                pltpu.VMEM((rows, width), jnp.bfloat16),
                pltpu.VMEM((rows, width), jnp.float32),
                pltpu.VMEM((rows, width), jnp.float32),
                pltpu.VMEM((rows, width), jnp.bfloat16),
                pltpu.VMEM((3 * rows, width), jnp.bfloat16),
                pltpu.VMEM((3 * rows, width), jnp.bfloat16),
                pltpu.VMEM((CHUNK, width), jnp.bfloat16),
                dma((2,)),
                dma((3 * parts,)),
                dma((3 * parts,)),
                dma((parts,)),
                dma((parts,)),
                dma((3 * parts,)),
                dma((3 * parts,)),
            ],
            compiler_params=pltpu.CompilerParams(
                collective_id=0, has_side_effects=True, vmem_limit_bytes=40 * 2**20),
        )(scale, bias, image, text)
        return both[0], both[1]

    in_specs = (P("blk", None), P("blk", None), P(), P())
    out_specs = (P("blk", None), P("blk", None))
    return jax.shard_map(local, mesh=mesh, in_specs=in_specs, out_specs=out_specs, check_vma=False)
```

```python
import functools

import jax
import jax.numpy as jnp
from jax import lax
from jax.experimental import pallas as pl
from jax.experimental.pallas import tpu as pltpu
from jax.sharding import PartitionSpec as P

MESH = pl.DeviceIdType.MESH
CHUNK = 128
EPS = 1e-06
MEBI = 2**20


def inverse_norm(wide):
    return lax.rsqrt(jnp.sum(wide * wide, axis=-1, keepdims=True) + EPS)


def norm_back(raw, grad):
    wide = raw.astype(jnp.float32)
    inverse = inverse_norm(wide)
    own = wide * inverse
    inner = jnp.sum(own * grad, axis=-1, keepdims=True)
    return (grad - own * inner) * inverse


def weigh(anchor, others, factor, offset, diagonal=False):
    logits = factor * lax.dot_general(
        anchor, others, (((1,), (1,)), ((), ())), preferred_element_type=jnp.float32) + offset
    probs = jax.nn.sigmoid(logits)
    if diagonal:
        row = lax.broadcasted_iota(jnp.int32, probs.shape, 0)
        column = lax.broadcasted_iota(jnp.int32, probs.shape, 1)
        probs = probs - (row == column).astype(jnp.float32)
    return (factor * probs).astype(jnp.bfloat16)


def low(raw):
    wide = raw.astype(jnp.float32)
    return (wide * inverse_norm(wide)).astype(jnp.bfloat16)


def exchange(n, scale_ref, bias_ref, image_ref, text_ref, x_raw, x_low, x_sum, y_grad, last, y_raw, y_low, y_sum,
             passed, near, far, unit, load_sem, link_send, link_recv, pass_send, pass_recv, pair_send, pair_recv):
    rows, width = x_raw.shape
    parts = rows // CHUNK
    me = lax.axis_index("blk")
    core = lax.rem(me, 2)
    partner = me + 1 - 2 * core
    ahead = lax.rem(me + 2 - 4 * core + n, n)
    behind = lax.rem(me - 2 + 4 * core + n, n)

    barrier = pltpu.get_barrier_semaphore()
    for other in (behind, partner):
        pl.semaphore_signal(barrier, inc=1, device_id=(other,), device_id_type=MESH)

    def load(x_ref, y_ref):
        pltpu.make_async_copy(y_ref, y_raw, load_sem.at[0]).start()
        pltpu.make_async_copy(x_ref, x_raw, load_sem.at[1]).start()

    pl.when(core == 0)(lambda: load(image_ref, text_ref))
    pl.when(core == 1)(lambda: load(text_ref, image_ref))

    factor = scale_ref[0]
    offset = bias_ref[0]

    def part(i):
        return pl.ds(i * CHUNK, CHUNK)

    def remote(src, dst, send, recv, device):
        return pltpu.make_async_remote_copy(
            src_ref=src, dst_ref=dst, send_sem=send, recv_sem=recv, device_id=(device,), device_id_type=MESH)

    def link(src, i):
        return remote(src, far.at[part(i)], link_send.at[i], link_recv.at[i], ahead)

    def hand(i):
        return remote(x_raw.at[part(i)], passed.at[part(i)], pass_send.at[i], pass_recv.at[i], partner)

    def pair(src, i):
        return remote(src, near.at[part(i)], pair_send.at[i], pair_recv.at[i], partner)

    pltpu.make_async_copy(text_ref, y_raw, load_sem.at[0]).wait()
    pltpu.make_async_copy(text_ref, x_raw, load_sem.at[1]).wait()
    pl.semaphore_wait(barrier, 2)
    link(y_raw.at[part(0)], 0).start()
    for i in range(parts):
        hand(i).start()
    for i in range(parts):
        pair(y_raw.at[part(i)], i).start()

    def lower(src, start, dst, count):
        @pl.loop(0, count)
        def _(i):
            dst[pl.ds(pl.multiple_of(i * CHUNK, CHUNK), CHUNK), :] = low(
                src[pl.ds(pl.multiple_of(start + i * CHUNK, CHUNK), CHUNK), :])

    def meet(anchor, src, start, total, count=parts):
        lower(src, start, unit, count)
        others = unit[pl.ds(0, count * CHUNK), :]
        weights = weigh(anchor[...], others, factor, offset)
        total[...] += jnp.dot(weights, others, preferred_element_type=jnp.float32)

    lower(x_raw, 0, x_low, parts)
    for i in range(parts):
        hand(i).wait_recv()
        link(passed.at[part(i)], 1 + i).start()
    for i in range(1, parts):
        link(y_raw.at[part(i)], parts + i).start()
    lower(y_raw, 0, y_low, parts)

    x_sum[...] = jnp.dot(
        weigh(x_low[...], y_low[...], factor, offset, True), y_low[...], preferred_element_type=jnp.float32)
    y_sum[...] = jnp.dot(
        weigh(y_low[...], x_low[...], factor, offset, True), x_low[...], preferred_element_type=jnp.float32)
    for i in range(parts):
        pair(y_raw.at[part(i)], i).wait_recv()
    meet(y_low, near, 0, y_sum)

    for block in range(2):
        for i in range(block * parts, (block + 1) * parts):
            link(y_raw.at[part(0)], i).wait_recv()
            pair(far.at[part(i)], i + parts).start()
            if 1 <= i <= parts:
                link(far.at[part(i)], i + 2 * parts - 1).start()
        meet(x_low, far, block * rows, x_sum)
        for i in range(block * parts, (block + 1) * parts):
            pair(far.at[part(i)], i + parts).wait_recv()
        meet(y_low, near, (block + 1) * rows, y_sum)

    @pl.loop(0, parts)
    def _(i):
        here = pl.ds(pl.multiple_of(i * CHUNK, CHUNK), CHUNK)
        y_grad[here, :] = norm_back(y_raw[here, :], y_sum[here, :])

    for i in range(2 * parts, 3 * parts - 1):
        link(y_raw.at[part(0)], i).wait_recv()
    meet(x_low, far, 2 * rows, x_sum, parts - 1)

    for i in range(parts):
        hand(i).wait_send()
    for i in range(3 * parts):
        pair(y_raw.at[part(0)], i).wait_send()
    for i in range(3 * parts):
        link(y_raw.at[part(0)], i).wait_send()
    link(y_raw.at[part(0)], 3 * parts - 1).wait_recv()
    last[...] = low(far[part(3 * parts - 1), :])


def conclude(scale_ref, bias_ref, x_raw, x_low, x_sum, y_grad, last, image_out, text_out, x_grad, weights, store_sem):
    rows, _ = x_raw.shape
    parts = rows // CHUNK
    core = lax.rem(lax.axis_index("blk"), 2)

    def store(src, out, i):
        return pltpu.make_async_copy(src, out, store_sem.at[i])

    for i in range(parts):
        here = pl.ds(i * CHUNK, CHUNK)
        pl.when(core == 0)(lambda: store(y_grad.at[here], text_out.at[here], parts + i).start())
        pl.when(core == 1)(lambda: store(y_grad.at[here], image_out.at[here], parts + i).start())
    weights[...] = weigh(x_low[...], last[...], scale_ref[0], bias_ref[0])
    for i in range(parts):
        here = pl.ds(i * CHUNK, CHUNK)
        grad = x_sum[here, :] + jnp.dot(weights[here, :], last[...], preferred_element_type=jnp.float32)
        x_grad[here, :] = norm_back(x_raw[here, :], grad)
        pl.when(core == 0)(lambda: store(x_grad.at[here], image_out.at[here], i).start())
        pl.when(core == 1)(lambda: store(x_grad.at[here], text_out.at[here], i).start())
    for i in range(parts):
        here = pl.ds(i * CHUNK, CHUNK)
        store(x_grad.at[here], image_out.at[here], i).wait()
        store(y_grad.at[here], text_out.at[here], parts + i).wait()


def solution(mesh):
    n = mesh.shape["blk"]

    def local(image, text, scale, bias):
        rows, width = image.shape
        parts = rows // CHUNK
        dma = pltpu.SemaphoreType.DMA
        half = pltpu.VMEM((rows, width), jnp.bfloat16)
        wide = pltpu.VMEM((rows, width), jnp.float32)
        piece = pltpu.VMEM((CHUNK, width), jnp.bfloat16)
        in_hbm = pl.BlockSpec(memory_space=pltpu.HBM)
        in_vmem = pl.BlockSpec(memory_space=pltpu.VMEM)
        in_smem = pl.BlockSpec(memory_space=pltpu.SMEM)
        held = pl.pallas_call(
            functools.partial(exchange, n),
            out_shape=(half, half, wide, wide, piece),
            in_specs=[in_smem] * 2 + [in_hbm] * 2,
            out_specs=(in_vmem,) * 5,
            scratch_shapes=[
                half, half, wide, half,
                pltpu.VMEM((3 * rows, width), jnp.bfloat16),
                pltpu.VMEM((3 * rows, width), jnp.bfloat16),
                half,
                dma((2,)),
                dma((3 * parts,)),
                dma((3 * parts,)),
                dma((parts,)),
                dma((parts,)),
                dma((3 * parts,)),
                dma((3 * parts,)),
            ],
            compiler_params=pltpu.CompilerParams(
                collective_id=0, has_side_effects=True, vmem_limit_bytes=40 * MEBI),
        )(scale, bias, pltpu.with_memory_space_constraint(image, pltpu.HBM),
          pltpu.with_memory_space_constraint(text, pltpu.HBM))
        out = jax.ShapeDtypeStruct((rows, width), jnp.float32)
        return pl.pallas_call(
            conclude,
            out_shape=(out, out),
            in_specs=[in_smem] * 2 + [in_vmem] * 5,
            out_specs=(in_hbm,) * 2,
            scratch_shapes=[wide, pltpu.VMEM((rows, CHUNK), jnp.bfloat16), dma((2 * parts,))],
            compiler_params=pltpu.CompilerParams(vmem_limit_bytes=16 * MEBI),
        )(scale, bias, *held)

    in_specs = (P("blk", None), P("blk", None), P(), P())
    out_specs = (P("blk", None), P("blk", None))
    return jax.shard_map(local, mesh=mesh, in_specs=in_specs, out_specs=out_specs, check_vma=False)
```

```python
import functools

import jax
import jax.numpy as jnp
from jax import lax
from jax.experimental import pallas as pl
from jax.experimental.pallas import tpu as pltpu
from jax.sharding import PartitionSpec as P

MESH = pl.DeviceIdType.MESH
CHUNK = 128
EPS = 1e-06
MEBI = 2**20
RING = 32


def inverse_norm(wide):
    return lax.rsqrt(jnp.sum(wide * wide, axis=-1, keepdims=True) + EPS)


def norm_back(raw, grad):
    wide = raw.astype(jnp.float32)
    inverse = inverse_norm(wide)
    own = wide * inverse
    inner = jnp.sum(own * grad, axis=-1, keepdims=True)
    return (grad - own * inner) * inverse


def weigh(anchor, others, factor, offset, diagonal=False):
    logits = factor * lax.dot_general(
        anchor, others, (((1,), (1,)), ((), ())), preferred_element_type=jnp.float32) + offset
    probs = jax.nn.sigmoid(logits)
    if diagonal:
        row = lax.broadcasted_iota(jnp.int32, probs.shape, 0)
        column = lax.broadcasted_iota(jnp.int32, probs.shape, 1)
        probs = probs - (row == column).astype(jnp.float32)
    return (factor * probs).astype(jnp.bfloat16)


def low(raw):
    wide = raw.astype(jnp.float32)
    return (wide * inverse_norm(wide)).astype(jnp.bfloat16)


def exchange(n, scale_ref, bias_ref, image_ref, text_ref, x_raw, x_low, x_sum, y_grad, last, y_raw, y_low, y_sum,
             passed, near, far, unit, load_sem, link_send, link_recv, pass_send, pass_recv, pair_send, pair_recv,
             help_send, go):
    rows, width = x_raw.shape
    parts = rows // CHUNK
    me = lax.axis_index("blk")
    core = lax.rem(me, 2)
    partner = me + 1 - 2 * core
    ahead = lax.rem(me + 2 - 4 * core + n, n)
    behind = lax.rem(me - 2 + 4 * core + n, n)
    chip = lax.rem(me // 2, RING)
    place = chip + core * (RING - 1 - 2 * chip)
    is_first = place == 0
    giver = (core == 1) & (place == RING - 1)
    helper = (core == 0) & is_first
    helped = (2, 3)

    barrier = pltpu.get_barrier_semaphore()
    for other in (behind, partner):
        pl.semaphore_signal(barrier, inc=1, device_id=(other,), device_id_type=MESH)

    def load(x_ref, y_ref):
        pltpu.make_async_copy(y_ref, y_raw, load_sem.at[0]).start()
        pltpu.make_async_copy(x_ref, x_raw, load_sem.at[1]).start()

    pl.when(core == 0)(lambda: load(image_ref, text_ref))
    pl.when(core == 1)(lambda: load(text_ref, image_ref))

    factor = scale_ref[0]
    offset = bias_ref[0]

    def part(i):
        return pl.ds(i * CHUNK, CHUNK)

    def remote(src, dst, send, recv, device):
        return pltpu.make_async_remote_copy(
            src_ref=src, dst_ref=dst, send_sem=send, recv_sem=recv, device_id=(device,), device_id_type=MESH)

    def link(src, i):
        return remote(src, far.at[part(i)], link_send.at[i], link_recv.at[i], ahead)

    def hand(src, i):
        return remote(src, passed.at[part(i)], pass_send.at[i], pass_recv.at[i], partner)

    def pair(src, i):
        return remote(src, near.at[part(i)], pair_send.at[i], pair_recv.at[i], partner)

    def help_out(k):
        i = 2 * parts + helped[k]
        return remote(near.at[part(parts + 1 + helped[k])], far.at[part(i)], help_send.at[k], link_recv.at[i],
                      lax.rem(me - 1 + n, n))

    pl.semaphore_wait(barrier, 2)

    def begin(x_ref, y_ref):
        link(y_ref.at[part(0)], 0).start()
        for i in range(parts):
            hand(x_ref.at[part(i)], i).start()

    pl.when(core == 0)(lambda: begin(image_ref, text_ref))
    pl.when(core == 1)(lambda: begin(text_ref, image_ref))

    pltpu.make_async_copy(text_ref, y_raw, load_sem.at[0]).wait()
    for i in range(parts):
        pair(y_raw.at[part(i)], i).start()

    @pl.when(giver)
    def _():
        pl.semaphore_signal(go, inc=1, device_id=(partner,), device_id_type=MESH)

    def own():
        for i in range(1, parts):
            link(y_raw.at[part(i)], parts + i).start()

    pl.when(is_first)(own)
    pltpu.make_async_copy(text_ref, x_raw, load_sem.at[1]).wait()

    def lower(src, start, dst, count):
        @pl.loop(0, count)
        def _(i):
            dst[pl.ds(pl.multiple_of(i * CHUNK, CHUNK), CHUNK), :] = low(
                src[pl.ds(pl.multiple_of(start + i * CHUNK, CHUNK), CHUNK), :])

    def meet(anchor, src, start, total, count=parts):
        lower(src, start, unit, count)
        others = unit[pl.ds(0, count * CHUNK), :]
        weights = weigh(anchor[...], others, factor, offset)
        total[...] += jnp.dot(weights, others, preferred_element_type=jnp.float32)

    lower(x_raw, 0, x_low, parts)
    for i in range(parts):
        hand(x_raw.at[part(i)], i).wait_recv()
        link(passed.at[part(i)], 1 + i).start()
    pl.when(jnp.logical_not(is_first))(own)
    lower(y_raw, 0, y_low, parts)

    x_sum[...] = jnp.dot(
        weigh(x_low[...], y_low[...], factor, offset, True), y_low[...], preferred_element_type=jnp.float32)
    y_sum[...] = jnp.dot(
        weigh(y_low[...], x_low[...], factor, offset, True), x_low[...], preferred_element_type=jnp.float32)
    for i in range(parts):
        pair(y_raw.at[part(i)], i).wait_recv()
    meet(y_low, near, 0, y_sum)

    for block in range(2):
        for i in range(block * parts, (block + 1) * parts):
            link(y_raw.at[part(0)], i).wait_recv()
            pair(far.at[part(i)], i + parts).start()
            if i - 1 in helped:
                pl.when(jnp.logical_not(giver))(lambda: link(far.at[part(i)], i + 2 * parts - 1).start())
            elif 1 <= i <= parts:
                link(far.at[part(i)], i + 2 * parts - 1).start()
        meet(x_low, far, block * rows, x_sum)
        for i in range(block * parts, (block + 1) * parts):
            pair(far.at[part(i)], i + parts).wait_recv()
        meet(y_low, near, (block + 1) * rows, y_sum)

    @pl.loop(0, parts)
    def _(i):
        here = pl.ds(pl.multiple_of(i * CHUNK, CHUNK), CHUNK)
        y_grad[here, :] = norm_back(y_raw[here, :], y_sum[here, :])

    @pl.when(helper)
    def _():
        pl.semaphore_wait(go, 1)
        for k in range(len(helped)):
            help_out(k).start()

    for i in range(2 * parts, 3 * parts - 1):
        link(y_raw.at[part(0)], i).wait_recv()
    meet(x_low, far, 2 * rows, x_sum, parts - 1)

    for i in range(parts):
        hand(x_raw.at[part(i)], i).wait_send()
    for i in range(3 * parts):
        pair(y_raw.at[part(0)], i).wait_send()
    for i in range(3 * parts):
        if i - 2 * parts in helped:
            pl.when(jnp.logical_not(giver))(lambda: link(y_raw.at[part(0)], i).wait_send())
        else:
            link(y_raw.at[part(0)], i).wait_send()
    link(y_raw.at[part(0)], 3 * parts - 1).wait_recv()
    last[...] = low(far[part(3 * parts - 1), :])

    @pl.when(helper)
    def _():
        for k in range(len(helped)):
            help_out(k).wait_send()


def conclude(scale_ref, bias_ref, x_raw, x_low, x_sum, y_grad, last, image_out, text_out, x_grad, weights, store_sem):
    rows, _ = x_raw.shape
    parts = rows // CHUNK
    core = lax.rem(lax.axis_index("blk"), 2)

    def store(src, out, i):
        return pltpu.make_async_copy(src, out, store_sem.at[i])

    for i in range(parts):
        here = pl.ds(i * CHUNK, CHUNK)
        pl.when(core == 0)(lambda: store(y_grad.at[here], text_out.at[here], parts + i).start())
        pl.when(core == 1)(lambda: store(y_grad.at[here], image_out.at[here], parts + i).start())
    weights[...] = weigh(x_low[...], last[...], scale_ref[0], bias_ref[0])
    for i in range(parts):
        here = pl.ds(i * CHUNK, CHUNK)
        grad = x_sum[here, :] + jnp.dot(weights[here, :], last[...], preferred_element_type=jnp.float32)
        x_grad[here, :] = norm_back(x_raw[here, :], grad)
        pl.when(core == 0)(lambda: store(x_grad.at[here], image_out.at[here], i).start())
        pl.when(core == 1)(lambda: store(x_grad.at[here], text_out.at[here], i).start())
    for i in range(parts):
        here = pl.ds(i * CHUNK, CHUNK)
        store(x_grad.at[here], image_out.at[here], i).wait()
        store(y_grad.at[here], text_out.at[here], parts + i).wait()


def solution(mesh):
    n = mesh.shape["blk"]

    def local(image, text, scale, bias):
        rows, width = image.shape
        parts = rows // CHUNK
        dma = pltpu.SemaphoreType.DMA
        half = pltpu.VMEM((rows, width), jnp.bfloat16)
        wide = pltpu.VMEM((rows, width), jnp.float32)
        piece = pltpu.VMEM((CHUNK, width), jnp.bfloat16)
        in_hbm = pl.BlockSpec(memory_space=pltpu.HBM)
        in_vmem = pl.BlockSpec(memory_space=pltpu.VMEM)
        in_smem = pl.BlockSpec(memory_space=pltpu.SMEM)
        held = pl.pallas_call(
            functools.partial(exchange, n),
            out_shape=(half, half, wide, wide, piece),
            in_specs=[in_smem] * 2 + [in_hbm] * 2,
            out_specs=(in_vmem,) * 5,
            scratch_shapes=[
                half, half, wide, half,
                pltpu.VMEM((3 * rows, width), jnp.bfloat16),
                pltpu.VMEM((3 * rows, width), jnp.bfloat16),
                half,
                dma((2,)),
                dma((3 * parts,)),
                dma((3 * parts,)),
                dma((parts,)),
                dma((parts,)),
                dma((3 * parts,)),
                dma((3 * parts,)),
                dma((2,)),
                pltpu.SemaphoreType.REGULAR,
            ],
            compiler_params=pltpu.CompilerParams(
                collective_id=0, has_side_effects=True, vmem_limit_bytes=40 * MEBI),
        )(scale, bias, pltpu.with_memory_space_constraint(image, pltpu.HBM),
          pltpu.with_memory_space_constraint(text, pltpu.HBM))
        out = jax.ShapeDtypeStruct((rows, width), jnp.float32)
        return pl.pallas_call(
            conclude,
            out_shape=(out, out),
            in_specs=[in_smem] * 2 + [in_vmem] * 5,
            out_specs=(in_hbm,) * 2,
            scratch_shapes=[wide, pltpu.VMEM((rows, CHUNK), jnp.bfloat16), dma((2 * parts,))],
            compiler_params=pltpu.CompilerParams(vmem_limit_bytes=16 * MEBI),
        )(scale, bias, *held)

    in_specs = (P("blk", None), P("blk", None), P(), P())
    out_specs = (P("blk", None), P("blk", None))
    return jax.shard_map(local, mesh=mesh, in_specs=in_specs, out_specs=out_specs, check_vma=False)
```

```python
import functools

import jax
import jax.numpy as jnp
from jax import lax
from jax.experimental import pallas as pl
from jax.experimental.pallas import tpu as pltpu
from jax.sharding import PartitionSpec as P

MESH = pl.DeviceIdType.MESH
CHUNK = 128
TILE = 128
EPS = 1e-06
MEBI = 2**20
RING = 32


def inverse_norm(wide):
    return lax.rsqrt(jnp.sum(wide * wide, axis=-1, keepdims=True) + EPS)


def norm_back(raw, grad):
    wide = raw.astype(jnp.float32)
    inverse = inverse_norm(wide)
    own = wide * inverse
    inner = jnp.sum(own * grad, axis=-1, keepdims=True)
    return (grad - own * inner) * inverse


def weigh(anchor, others, factor, offset, diagonal=False):
    logits = factor * lax.dot_general(
        anchor, others, (((1,), (1,)), ((), ())), preferred_element_type=jnp.float32) + offset
    probs = jax.nn.sigmoid(logits)
    if diagonal:
        row = lax.broadcasted_iota(jnp.int32, probs.shape, 0)
        column = lax.broadcasted_iota(jnp.int32, probs.shape, 1)
        probs = probs - (row == column).astype(jnp.float32)
    return (factor * probs).astype(jnp.bfloat16)


def low(raw):
    wide = raw.astype(jnp.float32)
    return (wide * inverse_norm(wide)).astype(jnp.bfloat16)


def exchange(n, scale_ref, bias_ref, image_ref, text_ref, x_low, x_unit, x_inverse, x_sum, y_grad, last, x_raw, y_raw,
             y_low, y_sum,
             passed, near, far, unit, load_sem, link_send, link_recv, pass_send, pass_recv, pair_send, pair_recv,
             help_send, go):
    rows, width = x_raw.shape
    parts = rows // CHUNK
    me = lax.axis_index("blk")
    core = lax.rem(me, 2)
    partner = me + 1 - 2 * core
    ahead = lax.rem(me + 2 - 4 * core + n, n)
    behind = lax.rem(me - 2 + 4 * core + n, n)
    chip = lax.rem(me // 2, RING)
    place = chip + core * (RING - 1 - 2 * chip)
    is_first = place == 0
    giver = (core == 1) & (place == RING - 1)
    helper = (core == 0) & is_first
    helped = (3,)

    barrier = pltpu.get_barrier_semaphore()
    for other in (behind, partner):
        pl.semaphore_signal(barrier, inc=1, device_id=(other,), device_id_type=MESH)

    def load(x_ref, y_ref):
        pltpu.make_async_copy(y_ref, y_raw, load_sem.at[0]).start()
        pltpu.make_async_copy(x_ref, x_raw, load_sem.at[1]).start()

    pl.when(core == 0)(lambda: load(image_ref, text_ref))
    pl.when(core == 1)(lambda: load(text_ref, image_ref))

    factor = scale_ref[0]
    offset = bias_ref[0]

    def part(i):
        return pl.ds(i * CHUNK, CHUNK)

    def remote(src, dst, send, recv, device):
        return pltpu.make_async_remote_copy(
            src_ref=src, dst_ref=dst, send_sem=send, recv_sem=recv, device_id=(device,), device_id_type=MESH)

    def link(src, i):
        return remote(src, far.at[part(i)], link_send.at[i], link_recv.at[i], ahead)

    def hand(src, i):
        return remote(src, passed.at[part(i)], pass_send.at[i], pass_recv.at[i], partner)

    def pair(src, i):
        return remote(src, near.at[part(i)], pair_send.at[i], pair_recv.at[i], partner)

    def help_out(k):
        i = 2 * parts + helped[k]
        return remote(near.at[part(parts + 1 + helped[k])], far.at[part(i)], help_send.at[k], link_recv.at[i],
                      lax.rem(me - 1 + n, n))

    pl.semaphore_wait(barrier, 2)

    def begin(x_ref, y_ref):
        link(y_ref.at[part(0)], 0).start()
        for i in range(parts):
            hand(x_ref.at[part(i)], i).start()

    pl.when(core == 0)(lambda: begin(image_ref, text_ref))
    pl.when(core == 1)(lambda: begin(text_ref, image_ref))

    pltpu.make_async_copy(text_ref, y_raw, load_sem.at[0]).wait()
    for i in range(parts):
        pair(y_raw.at[part(i)], i).start()

    @pl.when(giver)
    def _():
        pl.semaphore_signal(go, inc=1, device_id=(partner,), device_id_type=MESH)

    def own():
        for i in range(1, parts):
            link(y_raw.at[part(i)], parts + i).start()

    pl.when(is_first)(own)
    pltpu.make_async_copy(text_ref, x_raw, load_sem.at[1]).wait()

    def lower(src, start, dst, count):
        @pl.loop(0, count)
        def _(i):
            dst[pl.ds(pl.multiple_of(i * CHUNK, CHUNK), CHUNK), :] = low(
                src[pl.ds(pl.multiple_of(start + i * CHUNK, CHUNK), CHUNK), :])

    def meet(anchor, src, start, total, count=parts):
        lower(src, start, unit, count)
        others = unit[pl.ds(0, count * CHUNK), :]
        weights = weigh(anchor[...], others, factor, offset)
        total[...] += jnp.dot(weights, others, preferred_element_type=jnp.float32)

    lower(x_raw, 0, x_low, parts)
    for i in range(parts):
        hand(x_raw.at[part(i)], i).wait_recv()
        link(passed.at[part(i)], 1 + i).start()
    pl.when(jnp.logical_not(is_first))(own)
    lower(y_raw, 0, y_low, parts)

    x_sum[...] = jnp.dot(
        weigh(x_low[...], y_low[...], factor, offset, True), y_low[...], preferred_element_type=jnp.float32)
    y_sum[...] = jnp.dot(
        weigh(y_low[...], x_low[...], factor, offset, True), x_low[...], preferred_element_type=jnp.float32)
    for i in range(parts):
        pair(y_raw.at[part(i)], i).wait_recv()
    meet(y_low, near, 0, y_sum)

    for block in range(2):
        for i in range(block * parts, (block + 1) * parts):
            link(y_raw.at[part(0)], i).wait_recv()
            pair(far.at[part(i)], i + parts).start()
            if i - 1 in helped:
                pl.when(jnp.logical_not(giver))(lambda: link(far.at[part(i)], i + 2 * parts - 1).start())
            elif 1 <= i <= parts:
                link(far.at[part(i)], i + 2 * parts - 1).start()
        meet(x_low, far, block * rows, x_sum)
        for i in range(block * parts, (block + 1) * parts):
            pair(far.at[part(i)], i + parts).wait_recv()
        meet(y_low, near, (block + 1) * rows, y_sum)

    @pl.loop(0, parts)
    def _(i):
        here = pl.ds(pl.multiple_of(i * CHUNK, CHUNK), CHUNK)
        y_grad[here, :] = norm_back(y_raw[here, :], y_sum[here, :])
        wide = x_raw[here, :].astype(jnp.float32)
        inverse = inverse_norm(wide)
        x_inverse[here, :] = inverse
        x_unit[here, :] = wide * inverse

    @pl.when(helper)
    def _():
        pl.semaphore_wait(go, 1)
        for k in range(len(helped)):
            help_out(k).start()

    for i in range(2 * parts, 3 * parts - 1):
        link(y_raw.at[part(0)], i).wait_recv()
    meet(x_low, far, 2 * rows, x_sum, parts - 1)

    for i in range(parts):
        hand(x_raw.at[part(i)], i).wait_send()
    for i in range(3 * parts):
        pair(y_raw.at[part(0)], i).wait_send()
    for i in range(3 * parts):
        if i - 2 * parts in helped:
            pl.when(jnp.logical_not(giver))(lambda: link(y_raw.at[part(0)], i).wait_send())
        else:
            link(y_raw.at[part(0)], i).wait_send()
    link(y_raw.at[part(0)], 3 * parts - 1).wait_recv()
    last[...] = low(far[part(3 * parts - 1), :])

    @pl.when(helper)
    def _():
        for k in range(len(helped)):
            help_out(k).wait_send()


def conclude(scale_ref, bias_ref, x_low, x_unit, x_inverse, x_sum, y_grad, last, image_out, text_out, x_grad, weights, store_sem):
    rows, _ = x_low.shape
    parts = rows // CHUNK
    core = lax.rem(lax.axis_index("blk"), 2)

    def store(src, out, i):
        return pltpu.make_async_copy(src, out, store_sem.at[i])

    for i in range(parts):
        here = pl.ds(i * CHUNK, CHUNK)
        pl.when(core == 0)(lambda: store(y_grad.at[here], text_out.at[here], parts + i).start())
        pl.when(core == 1)(lambda: store(y_grad.at[here], image_out.at[here], parts + i).start())
    weights[...] = weigh(x_low[...], last[...], scale_ref[0], bias_ref[0])
    tiles = rows // TILE
    for i in range(tiles):
        here = pl.ds(i * TILE, TILE)
        grad = x_sum[here, :] + jnp.dot(weights[here, :], last[...], preferred_element_type=jnp.float32)
        own = x_unit[here, :]
        inner = jnp.sum(own * grad, axis=-1, keepdims=True)
        x_grad[here, :] = (grad - own * inner) * x_inverse[here, :]
        pl.when(core == 0)(lambda: store(x_grad.at[here], image_out.at[here], 2 * parts + i).start())
        pl.when(core == 1)(lambda: store(x_grad.at[here], text_out.at[here], 2 * parts + i).start())
    for i in range(parts):
        here = pl.ds(i * CHUNK, CHUNK)
        store(y_grad.at[here], text_out.at[here], parts + i).wait()
    for i in range(tiles):
        here = pl.ds(i * TILE, TILE)
        store(x_grad.at[here], image_out.at[here], 2 * parts + i).wait()


def solution(mesh):
    n = mesh.shape["blk"]

    def local(image, text, scale, bias):
        rows, width = image.shape
        parts = rows // CHUNK
        dma = pltpu.SemaphoreType.DMA
        half = pltpu.VMEM((rows, width), jnp.bfloat16)
        wide = pltpu.VMEM((rows, width), jnp.float32)
        piece = pltpu.VMEM((CHUNK, width), jnp.bfloat16)
        in_hbm = pl.BlockSpec(memory_space=pltpu.HBM)
        in_vmem = pl.BlockSpec(memory_space=pltpu.VMEM)
        in_smem = pl.BlockSpec(memory_space=pltpu.SMEM)
        held = pl.pallas_call(
            functools.partial(exchange, n),
            out_shape=(half, wide, pltpu.VMEM((rows, 1), jnp.float32), wide, wide, piece),
            in_specs=[in_smem] * 2 + [in_hbm] * 2,
            out_specs=(in_vmem,) * 6,
            scratch_shapes=[
                half, half, half, wide, half,
                pltpu.VMEM((3 * rows, width), jnp.bfloat16),
                pltpu.VMEM((3 * rows, width), jnp.bfloat16),
                half,
                dma((2,)),
                dma((3 * parts,)),
                dma((3 * parts,)),
                dma((parts,)),
                dma((parts,)),
                dma((3 * parts,)),
                dma((3 * parts,)),
                dma((1,)),
                pltpu.SemaphoreType.REGULAR,
            ],
            compiler_params=pltpu.CompilerParams(
                collective_id=0, has_side_effects=True, vmem_limit_bytes=40 * MEBI),
        )(scale, bias, pltpu.with_memory_space_constraint(image, pltpu.HBM),
          pltpu.with_memory_space_constraint(text, pltpu.HBM))
        out = jax.ShapeDtypeStruct((rows, width), jnp.float32)
        return pl.pallas_call(
            conclude,
            out_shape=(out, out),
            in_specs=[in_smem] * 2 + [in_vmem] * 6,
            out_specs=(in_hbm,) * 2,
            scratch_shapes=[wide, pltpu.VMEM((rows, CHUNK), jnp.bfloat16), dma((2 * parts + rows // TILE,))],
            compiler_params=pltpu.CompilerParams(vmem_limit_bytes=16 * MEBI),
        )(scale, bias, *held)

    in_specs = (P("blk", None), P("blk", None), P(), P())
    out_specs = (P("blk", None), P("blk", None))
    return jax.shard_map(local, mesh=mesh, in_specs=in_specs, out_specs=out_specs, check_vma=False)
```

```python
import functools

import jax
import jax.numpy as jnp
from jax import lax
from jax.experimental import pallas as pl
from jax.experimental.pallas import tpu as pltpu
from jax.sharding import PartitionSpec as P

MESH = pl.DeviceIdType.MESH
CHUNK = 128
EPS = 1e-06
MEBI = 2**20
RING = 32


def inverse_norm(wide):
    return lax.rsqrt(jnp.sum(wide * wide, axis=-1, keepdims=True) + EPS)


def norm_back(raw, grad):
    wide = raw.astype(jnp.float32)
    inverse = inverse_norm(wide)
    own = wide * inverse
    inner = jnp.sum(own * grad, axis=-1, keepdims=True)
    return (grad - own * inner) * inverse


def weigh(anchor, others, factor, offset, diagonal=False):
    logits = factor * lax.dot_general(
        anchor, others, (((1,), (1,)), ((), ())), preferred_element_type=jnp.float32) + offset
    probs = jax.nn.sigmoid(logits)
    if diagonal:
        row = lax.broadcasted_iota(jnp.int32, probs.shape, 0)
        column = lax.broadcasted_iota(jnp.int32, probs.shape, 1)
        probs = probs - (row == column).astype(jnp.float32)
    return (factor * probs).astype(jnp.bfloat16)


def low(raw):
    wide = raw.astype(jnp.float32)
    return (wide * inverse_norm(wide)).astype(jnp.bfloat16)


def exchange(n, scale_ref, bias_ref, image_ref, text_ref, x_low, x_unit, x_inverse, x_sum, y_grad, last, x_raw, y_raw,
             y_low, y_sum,
             passed, near, far, unit, load_sem, link_send, link_recv, pass_send, pass_recv, pair_send, pair_recv,
             help_send, go):
    rows, width = x_raw.shape
    parts = rows // CHUNK
    me = lax.axis_index("blk")
    core = lax.rem(me, 2)
    partner = me + 1 - 2 * core
    ahead = lax.rem(me + 2 - 4 * core + n, n)
    behind = lax.rem(me - 2 + 4 * core + n, n)
    chip = lax.rem(me // 2, RING)
    place = chip + core * (RING - 1 - 2 * chip)
    is_first = place == 0
    giver = (core == 1) & (place == RING - 1)
    helper = (core == 0) & is_first
    helped = (3,)

    barrier = pltpu.get_barrier_semaphore()
    for other in (behind, partner):
        pl.semaphore_signal(barrier, inc=1, device_id=(other,), device_id_type=MESH)

    factor = scale_ref[0]
    offset = bias_ref[0]

    def part(i):
        return pl.ds(i * CHUNK, CHUNK)

    def remote(src, dst, send, recv, device):
        return pltpu.make_async_remote_copy(
            src_ref=src, dst_ref=dst, send_sem=send, recv_sem=recv, device_id=(device,), device_id_type=MESH)

    def link(src, i):
        return remote(src, far.at[part(i)], link_send.at[i], link_recv.at[i], ahead)

    def hand(src, i):
        return remote(src, passed.at[part(i)], pass_send.at[i], pass_recv.at[i], partner)

    def pair(src, i):
        return remote(src, near.at[part(i)], pair_send.at[i], pair_recv.at[i], partner)

    def help_out(k):
        i = 2 * parts + helped[k]
        return remote(near.at[part(parts + 1 + helped[k])], far.at[part(i)], help_send.at[k], link_recv.at[i],
                      lax.rem(me - 1 + n, n))

    pl.semaphore_wait(barrier, 2)

    def begin(x_ref, y_ref):
        link(y_ref.at[part(0)], 0).start()
        for i in range(parts):
            hand(x_ref.at[part(i)], i).start()
        pltpu.make_async_copy(y_ref, y_raw, load_sem.at[0]).start()
        pltpu.make_async_copy(x_ref, x_raw, load_sem.at[1]).start()

    pl.when(core == 0)(lambda: begin(image_ref, text_ref))
    pl.when(core == 1)(lambda: begin(text_ref, image_ref))

    pltpu.make_async_copy(text_ref, y_raw, load_sem.at[0]).wait()
    for i in range(parts):
        pair(y_raw.at[part(i)], i).start()

    @pl.when(giver)
    def _():
        pl.semaphore_signal(go, inc=1, device_id=(partner,), device_id_type=MESH)

    def own():
        for i in range(1, parts):
            link(y_raw.at[part(i)], parts + i).start()

    pl.when(is_first)(own)
    pltpu.make_async_copy(text_ref, x_raw, load_sem.at[1]).wait()

    def lower(src, start, dst, count):
        @pl.loop(0, count)
        def _(i):
            dst[pl.ds(pl.multiple_of(i * CHUNK, CHUNK), CHUNK), :] = low(
                src[pl.ds(pl.multiple_of(start + i * CHUNK, CHUNK), CHUNK), :])

    def meet(anchor, src, start, total, count=parts):
        lower(src, start, unit, count)
        others = unit[pl.ds(0, count * CHUNK), :]
        weights = weigh(anchor[...], others, factor, offset)
        total[...] += jnp.dot(weights, others, preferred_element_type=jnp.float32)

    lower(x_raw, 0, x_low, parts)
    for i in range(parts):
        hand(x_raw.at[part(i)], i).wait_recv()
        link(passed.at[part(i)], 1 + i).start()
    pl.when(jnp.logical_not(is_first))(own)
    lower(y_raw, 0, y_low, parts)

    x_sum[...] = jnp.dot(
        weigh(x_low[...], y_low[...], factor, offset, True), y_low[...], preferred_element_type=jnp.float32)
    y_sum[...] = jnp.dot(
        weigh(y_low[...], x_low[...], factor, offset, True), x_low[...], preferred_element_type=jnp.float32)
    for i in range(parts):
        pair(y_raw.at[part(i)], i).wait_recv()
    meet(y_low, near, 0, y_sum)

    for block in range(2):
        for i in range(block * parts, (block + 1) * parts):
            link(y_raw.at[part(0)], i).wait_recv()
            pair(far.at[part(i)], i + parts).start()
            if i - 1 in helped:
                pl.when(jnp.logical_not(giver))(lambda: link(far.at[part(i)], i + 2 * parts - 1).start())
            elif 1 <= i <= parts:
                link(far.at[part(i)], i + 2 * parts - 1).start()
        meet(x_low, far, block * rows, x_sum)
        for i in range(block * parts, (block + 1) * parts):
            pair(far.at[part(i)], i + parts).wait_recv()
        meet(y_low, near, (block + 1) * rows, y_sum)

    @pl.loop(0, parts)
    def _(i):
        here = pl.ds(pl.multiple_of(i * CHUNK, CHUNK), CHUNK)
        y_grad[here, :] = norm_back(y_raw[here, :], y_sum[here, :])
        wide = x_raw[here, :].astype(jnp.float32)
        inverse = inverse_norm(wide)
        x_inverse[here, :] = inverse
        x_unit[here, :] = wide * inverse

    @pl.when(helper)
    def _():
        pl.semaphore_wait(go, 1)
        for k in range(len(helped)):
            help_out(k).start()

    for i in range(2 * parts, 3 * parts - 1):
        link(y_raw.at[part(0)], i).wait_recv()
    meet(x_low, far, 2 * rows, x_sum, parts - 1)

    for i in range(parts):
        hand(x_raw.at[part(i)], i).wait_send()
    for i in range(3 * parts):
        pair(y_raw.at[part(0)], i).wait_send()
    for i in range(3 * parts):
        if i - 2 * parts in helped:
            pl.when(jnp.logical_not(giver))(lambda: link(y_raw.at[part(0)], i).wait_send())
        else:
            link(y_raw.at[part(0)], i).wait_send()
    link(y_raw.at[part(0)], 3 * parts - 1).wait_recv()
    last[...] = low(far[part(3 * parts - 1), :])

    @pl.when(helper)
    def _():
        for k in range(len(helped)):
            help_out(k).wait_send()


def conclude(scale_ref, bias_ref, x_low, x_unit, x_inverse, x_sum, y_grad, last, image_out, text_out, x_grad, weights, store_sem):
    rows, _ = x_low.shape
    parts = rows // CHUNK
    core = lax.rem(lax.axis_index("blk"), 2)

    def store(src, out, i):
        return pltpu.make_async_copy(src, out, store_sem.at[i])

    def run(x_out, y_out):
        for i in range(parts):
            here = pl.ds(i * CHUNK, CHUNK)
            store(y_grad.at[here], y_out.at[here], parts + i).start()
        weights[...] = weigh(x_low[...], last[...], scale_ref[0], bias_ref[0])
        for i in range(parts):
            here = pl.ds(i * CHUNK, CHUNK)
            grad = x_sum[here, :] + jnp.dot(weights[here, :], last[...], preferred_element_type=jnp.float32)
            own = x_unit[here, :]
            inner = jnp.sum(own * grad, axis=-1, keepdims=True)
            x_grad[here, :] = (grad - own * inner) * x_inverse[here, :]
            store(x_grad.at[here], x_out.at[here], i).start()
        for i in range(parts):
            here = pl.ds(i * CHUNK, CHUNK)
            store(y_grad.at[here], y_out.at[here], parts + i).wait()
            store(x_grad.at[here], x_out.at[here], i).wait()

    pl.when(core == 0)(lambda: run(image_out, text_out))
    pl.when(core == 1)(lambda: run(text_out, image_out))


def solution(mesh):
    n = mesh.shape["blk"]

    def local(image, text, scale, bias):
        rows, width = image.shape
        parts = rows // CHUNK
        dma = pltpu.SemaphoreType.DMA
        half = pltpu.VMEM((rows, width), jnp.bfloat16)
        wide = pltpu.VMEM((rows, width), jnp.float32)
        piece = pltpu.VMEM((CHUNK, width), jnp.bfloat16)
        in_hbm = pl.BlockSpec(memory_space=pltpu.HBM)
        in_vmem = pl.BlockSpec(memory_space=pltpu.VMEM)
        in_smem = pl.BlockSpec(memory_space=pltpu.SMEM)
        held = pl.pallas_call(
            functools.partial(exchange, n),
            out_shape=(half, wide, pltpu.VMEM((rows, 1), jnp.float32), wide, wide, piece),
            in_specs=[in_smem] * 2 + [in_hbm] * 2,
            out_specs=(in_vmem,) * 6,
            scratch_shapes=[
                half, half, half, wide, half,
                pltpu.VMEM((3 * rows, width), jnp.bfloat16),
                pltpu.VMEM((3 * rows, width), jnp.bfloat16),
                half,
                dma((2,)),
                dma((3 * parts,)),
                dma((3 * parts,)),
                dma((parts,)),
                dma((parts,)),
                dma((3 * parts,)),
                dma((3 * parts,)),
                dma((1,)),
                pltpu.SemaphoreType.REGULAR,
            ],
            compiler_params=pltpu.CompilerParams(
                collective_id=0, has_side_effects=True, vmem_limit_bytes=40 * MEBI),
        )(scale, bias, pltpu.with_memory_space_constraint(image, pltpu.HBM),
          pltpu.with_memory_space_constraint(text, pltpu.HBM))
        out = jax.ShapeDtypeStruct((rows, width), jnp.float32)
        return pl.pallas_call(
            conclude,
            out_shape=(out, out),
            in_specs=[in_smem] * 2 + [in_vmem] * 6,
            out_specs=(in_hbm,) * 2,
            scratch_shapes=[wide, pltpu.VMEM((rows, CHUNK), jnp.bfloat16), dma((2 * parts,))],
            compiler_params=pltpu.CompilerParams(vmem_limit_bytes=16 * MEBI),
        )(scale, bias, *held)

    in_specs = (P("blk", None), P("blk", None), P(), P())
    out_specs = (P("blk", None), P("blk", None))
    return jax.shard_map(local, mesh=mesh, in_specs=in_specs, out_specs=out_specs, check_vma=False)
```

```python
import functools

import jax
import jax.numpy as jnp
from jax import lax
from jax.experimental import pallas as pl
from jax.experimental.pallas import tpu as pltpu
from jax.sharding import PartitionSpec as P

MESH = pl.DeviceIdType.MESH
CHUNK = 128
EPS = 1e-06
MEBI = 2**20
RING = 32


def inverse_norm(wide):
    return lax.rsqrt(jnp.sum(wide * wide, axis=-1, keepdims=True) + EPS)


def norm_back(raw, grad):
    wide = raw.astype(jnp.float32)
    inverse = inverse_norm(wide)
    own = wide * inverse
    inner = jnp.sum(own * grad, axis=-1, keepdims=True)
    return (grad - own * inner) * inverse


def weigh(anchor, others, factor, offset, diagonal=False):
    logits = factor * lax.dot_general(
        anchor, others, (((1,), (1,)), ((), ())), preferred_element_type=jnp.float32) + offset
    probs = jax.nn.sigmoid(logits)
    if diagonal:
        row = lax.broadcasted_iota(jnp.int32, probs.shape, 0)
        column = lax.broadcasted_iota(jnp.int32, probs.shape, 1)
        probs = probs - (row == column).astype(jnp.float32)
    return (factor * probs).astype(jnp.bfloat16)


def low(raw):
    wide = raw.astype(jnp.float32)
    return (wide * inverse_norm(wide)).astype(jnp.bfloat16)


def exchange(n, scale_ref, bias_ref, image_ref, text_ref, x_low, x_unit, x_inverse, x_sum, y_grad, last, x_raw, y_raw,
             y_low, y_sum,
             passed, near, far, unit, load_sem, link_send, link_recv, pass_send, pass_recv, pair_send, pair_recv,
             help_send, go):
    rows, width = x_raw.shape
    parts = rows // CHUNK
    me = lax.axis_index("blk")
    core = lax.rem(me, 2)
    partner = me + 1 - 2 * core
    ahead = lax.rem(me + 2 - 4 * core + n, n)
    behind = lax.rem(me - 2 + 4 * core + n, n)
    chip = lax.rem(me // 2, RING)
    place = chip + core * (RING - 1 - 2 * chip)
    is_first = place == 0
    giver = (core == 1) & (place == RING - 1)
    helper = (core == 0) & is_first
    helped = (3,)

    barrier = pltpu.get_barrier_semaphore()
    for other in (behind, partner):
        pl.semaphore_signal(barrier, inc=1, device_id=(other,), device_id_type=MESH)

    factor = scale_ref[0]
    offset = bias_ref[0]

    def part(i):
        return pl.ds(i * CHUNK, CHUNK)

    def remote(src, dst, send, recv, device):
        return pltpu.make_async_remote_copy(
            src_ref=src, dst_ref=dst, send_sem=send, recv_sem=recv, device_id=(device,), device_id_type=MESH)

    def link(src, i):
        return remote(src, far.at[part(i)], link_send.at[i], link_recv.at[i], ahead)

    def hand(src, i):
        return remote(src, passed.at[part(i)], pass_send.at[i], pass_recv.at[i], partner)

    def pair(src, i):
        return remote(src, near.at[part(i)], pair_send.at[i], pair_recv.at[i], partner)

    def help_out(k):
        i = 2 * parts + helped[k]
        return remote(near.at[part(parts + 1 + helped[k])], far.at[part(i)], help_send.at[k], link_recv.at[i],
                      lax.rem(me - 1 + n, n))

    pl.semaphore_wait(barrier, 2)

    def begin(x_ref, y_ref):
        link(y_ref.at[part(0)], 0).start()
        for i in range(parts):
            hand(x_ref.at[part(i)], i).start()
        pltpu.make_async_copy(y_ref, y_raw, load_sem.at[0]).start()
        pltpu.make_async_copy(x_ref, x_raw, load_sem.at[1]).start()

    pl.when(core == 0)(lambda: begin(image_ref, text_ref))
    pl.when(core == 1)(lambda: begin(text_ref, image_ref))

    pltpu.make_async_copy(text_ref, y_raw, load_sem.at[0]).wait()
    for i in range(parts):
        pair(y_raw.at[part(i)], i).start()

    @pl.when(giver)
    def _():
        pl.semaphore_signal(go, inc=1, device_id=(partner,), device_id_type=MESH)

    def own():
        for i in range(1, parts):
            link(y_raw.at[part(i)], parts + i).start()

    pl.when(is_first)(own)
    pltpu.make_async_copy(text_ref, x_raw, load_sem.at[1]).wait()

    def lower(src, start, dst, count):
        @pl.loop(0, count)
        def _(i):
            dst[pl.ds(pl.multiple_of(i * CHUNK, CHUNK), CHUNK), :] = low(
                src[pl.ds(pl.multiple_of(start + i * CHUNK, CHUNK), CHUNK), :])

    def meet(anchor, src, start, total, count=parts):
        lower(src, start, unit, count)
        others = unit[pl.ds(0, count * CHUNK), :]
        weights = weigh(anchor[...], others, factor, offset)
        total[...] += jnp.dot(weights, others, preferred_element_type=jnp.float32)

    lower(x_raw, 0, x_low, parts)
    for i in range(parts):
        hand(x_raw.at[part(i)], i).wait_recv()
        link(passed.at[part(i)], 1 + i).start()
    pl.when(jnp.logical_not(is_first))(own)
    lower(y_raw, 0, y_low, parts)

    x_sum[...] = jnp.dot(
        weigh(x_low[...], y_low[...], factor, offset, True), y_low[...], preferred_element_type=jnp.float32)
    y_sum[...] = jnp.dot(
        weigh(y_low[...], x_low[...], factor, offset, True), x_low[...], preferred_element_type=jnp.float32)
    for i in range(parts):
        pair(y_raw.at[part(i)], i).wait_recv()
    meet(y_low, near, 0, y_sum)

    for block in range(2):
        for i in range(block * parts, (block + 1) * parts):
            link(y_raw.at[part(0)], i).wait_recv()
            pair(far.at[part(i)], i + parts).start()
            if i - 1 in helped:
                pl.when(jnp.logical_not(giver))(lambda: link(far.at[part(i)], i + 2 * parts - 1).start())
            elif 1 <= i <= parts:
                link(far.at[part(i)], i + 2 * parts - 1).start()
        meet(x_low, far, block * rows, x_sum)
        for i in range(block * parts, (block + 1) * parts):
            pair(far.at[part(i)], i + parts).wait_recv()
        meet(y_low, near, (block + 1) * rows, y_sum)

    @pl.loop(0, parts)
    def _(i):
        here = pl.ds(pl.multiple_of(i * CHUNK, CHUNK), CHUNK)
        y_grad[here, :] = norm_back(y_raw[here, :], y_sum[here, :])
        wide = x_raw[here, :].astype(jnp.float32)
        inverse = inverse_norm(wide)
        x_inverse[here, :] = inverse
        x_unit[here, :] = wide * inverse

    @pl.when(helper)
    def _():
        pl.semaphore_wait(go, 1)
        for k in range(len(helped)):
            help_out(k).start()

    for i in range(2 * parts, 3 * parts - 1):
        link(y_raw.at[part(0)], i).wait_recv()
    meet(x_low, far, 2 * rows, x_sum, parts - 1)

    for i in range(parts):
        hand(x_raw.at[part(i)], i).wait_send()
    for i in range(3 * parts):
        pair(y_raw.at[part(0)], i).wait_send()
    for i in range(3 * parts):
        if i - 2 * parts in helped:
            pl.when(jnp.logical_not(giver))(lambda: link(y_raw.at[part(0)], i).wait_send())
        else:
            link(y_raw.at[part(0)], i).wait_send()
    link(y_raw.at[part(0)], 3 * parts - 1).wait_recv()
    last[...] = low(far[part(3 * parts - 1), :])

    @pl.when(helper)
    def _():
        for k in range(len(helped)):
            help_out(k).wait_send()


def conclude(scale_ref, bias_ref, x_low, x_unit, x_inverse, x_sum, y_grad, last, image_out, text_out, x_grad, weights, store_sem):
    rows, _ = x_low.shape
    parts = rows // CHUNK
    core = lax.rem(lax.axis_index("blk"), 2)

    def store(src, out, i):
        return pltpu.make_async_copy(src, out, store_sem.at[i])

    def run(x_out, y_out):
        store(y_grad, y_out, parts).start()
        weights[...] = weigh(x_low[...], last[...], scale_ref[0], bias_ref[0])
        for i in range(parts):
            here = pl.ds(i * CHUNK, CHUNK)
            grad = x_sum[here, :] + jnp.dot(weights[here, :], last[...], preferred_element_type=jnp.float32)
            own = x_unit[here, :]
            inner = jnp.sum(own * grad, axis=-1, keepdims=True)
            x_grad[here, :] = (grad - own * inner) * x_inverse[here, :]
            store(x_grad.at[here], x_out.at[here], i).start()
        for i in range(parts):
            here = pl.ds(i * CHUNK, CHUNK)
            store(x_grad.at[here], x_out.at[here], i).wait()
        store(y_grad, y_out, parts).wait()

    pl.when(core == 0)(lambda: run(image_out, text_out))
    pl.when(core == 1)(lambda: run(text_out, image_out))


def solution(mesh):
    n = mesh.shape["blk"]

    def local(image, text, scale, bias):
        rows, width = image.shape
        parts = rows // CHUNK
        dma = pltpu.SemaphoreType.DMA
        half = pltpu.VMEM((rows, width), jnp.bfloat16)
        wide = pltpu.VMEM((rows, width), jnp.float32)
        piece = pltpu.VMEM((CHUNK, width), jnp.bfloat16)
        in_hbm = pl.BlockSpec(memory_space=pltpu.HBM)
        in_vmem = pl.BlockSpec(memory_space=pltpu.VMEM)
        in_smem = pl.BlockSpec(memory_space=pltpu.SMEM)
        held = pl.pallas_call(
            functools.partial(exchange, n),
            out_shape=(half, wide, pltpu.VMEM((rows, 1), jnp.float32), wide, wide, piece),
            in_specs=[in_smem] * 2 + [in_hbm] * 2,
            out_specs=(in_vmem,) * 6,
            scratch_shapes=[
                half, half, half, wide, half,
                pltpu.VMEM((3 * rows, width), jnp.bfloat16),
                pltpu.VMEM((3 * rows, width), jnp.bfloat16),
                half,
                dma((2,)),
                dma((3 * parts,)),
                dma((3 * parts,)),
                dma((parts,)),
                dma((parts,)),
                dma((3 * parts,)),
                dma((3 * parts,)),
                dma((1,)),
                pltpu.SemaphoreType.REGULAR,
            ],
            compiler_params=pltpu.CompilerParams(
                collective_id=0, has_side_effects=True, vmem_limit_bytes=40 * MEBI),
        )(scale, bias, pltpu.with_memory_space_constraint(image, pltpu.HBM),
          pltpu.with_memory_space_constraint(text, pltpu.HBM))
        out = jax.ShapeDtypeStruct((rows, width), jnp.float32)
        return pl.pallas_call(
            conclude,
            out_shape=(out, out),
            in_specs=[in_smem] * 2 + [in_vmem] * 6,
            out_specs=(in_hbm,) * 2,
            scratch_shapes=[wide, pltpu.VMEM((rows, CHUNK), jnp.bfloat16), dma((parts + 1,))],
            compiler_params=pltpu.CompilerParams(vmem_limit_bytes=16 * MEBI),
        )(scale, bias, *held)

    in_specs = (P("blk", None), P("blk", None), P(), P())
    out_specs = (P("blk", None), P("blk", None))
    return jax.shard_map(local, mesh=mesh, in_specs=in_specs, out_specs=out_specs, check_vma=False)
```
